512 devices in a mesh: expert: 128 (over y, z, core), dp: 4 (over x).
Axes of the slice: x: 4, y: 4, z: 16, core: 2. Of those that a mesh axis runs over, the one named last changes fastest.
Arguments:
- tokens: bfloat16 [65536, 2048], P(('expert', 'dp')), may hold values from -6 to 6
- cotangent: bfloat16 [65536, 8, 384], P(('expert', 'dp')), may hold values from -3 to 3
- routes: int32 [65536, 8], P(('expert', 'dp')), may hold values from 0 to 127, all different within a row
- route_weight: float32 [65536, 8], P(('expert', 'dp')), may hold values from 0.05 to 1
- expert_slot: int32 [128], replicated, may hold values from 0 to 127, each once
- capacity: int32 [128], replicated, may hold values from 2 to 6, as said below
- gate_up: bfloat16 [128, 2048, 768], P('expert', 'dp'), may hold values from -0.125 to 0.125
Outputs:
- token_grad: bfloat16 [65536, 2048], P(('expert', 'dp'))
- route_weight_grad: float32 [65536, 8], P(('expert', 'dp'))
- gate_up_grad: bfloat16 [128, 2048, 768], P('expert', 'dp')
The draws below stay inside these ranges and needn't reach their ends.
Inputs may be any that keep to these rules, and one draw needn't show every extreme that they name: Every capacity is even; capacity[d] + capacity[(d + 64) mod 128] <= 8 for every slot d; some slot has exactly 6.
All inputs are finite; a program needn't handle non-finite values.
Results may differ from the reference program's by a relative error of at most 0.02.
Values may be sent and summed in bfloat16 or wider, within the bound.
No kernel may reach another device: no remote copies, remote signals or barrier semaphores. Data moves between devices by JAX's collectives and lax.ppermute only.
A program may use at most 64 MiB of HBM per device.

```python
import math
import jax
import jax.numpy as jnp
from jax import lax

D = 2048
I = 384
TOP = 8
CAP = 6
TOK_DEV = 128
EXPERTS = 128
TOKENS = 65536
N_EXPERT = 128
N_DP = 4


def draw_capacity(key, part):
    half_count = EXPERTS // 2
    even_share = (CAP + 2) // 2
    pattern = jax.random.randint(key, (half_count,), 0, 3)
    pattern = pattern.at[0].set(0)
    first_half = jnp.where(pattern == 0, CAP, jnp.where(pattern == 1, 2, even_share))
    second_half = jnp.where(pattern == 1, CAP, jnp.where(pattern == 0, 2, even_share))
    return jnp.concatenate([first_half, second_half]).astype(jnp.int32)


def steps_of(rng, shape, cuts, least, largest):
    def one(dim, shards_of):
        draws = jax.random.uniform(jax.random.fold_in(jax.random.fold_in(rng, 6), dim), (shards_of,), jnp.float32, least / len(cuts), largest / len(cuts))
        return jnp.repeat(jnp.exp(draws), shape[dim] // shards_of).reshape((-1,) + (1,) * (len(shape) - dim - 1))

    gain = one(*cuts[0])
    for cut in cuts[1:]:
        gain = gain * one(*cut)
    return gain


def choose_distinct(stream_key, rows, count, top, lift):
    order = jax.random.permutation(jax.random.fold_in(stream_key, 1), count)
    favour = order
    for power in range(3):
        favour = favour * favour // count
    favour = favour * lift // count
    lots = jax.random.randint(jax.random.fold_in(stream_key, 2), (rows, count), 0, 4096) + favour
    holders = jax.random.permutation(jax.random.fold_in(stream_key, 3), rows)[jnp.arange(count) % rows]
    lots = jnp.where(jnp.arange(rows)[:, None] == holders[None, :], 1 << 14, lots)
    merit = lots * count + jnp.arange(count)
    return lax.top_k(merit.astype(jnp.int32), top)[1].astype(jnp.int32)


def bell_draw(rng, extent, spread, bound, split=(), kind=jnp.bfloat16):
    result = jax.random.normal(rng, extent, jnp.float32) * spread
    if len(split) > 0:
        result = steps_of(rng, extent, split, -0.22, 0.18) * result
    return jnp.clip(result, min=-bound, max=bound).astype(kind)


def setup_inputs(seed: int = 0) -> dict:
    key_list = jax.random.split(jax.random.key(seed), 8)
    tokens = bell_draw(key_list[0], (TOKENS, D), 1.0, 6.0, ((0, 512),))
    cotangent = bell_draw(key_list[1], (TOKENS, TOP, I), 0.5, 3.0, ((0, 512),))
    routes = choose_distinct(key_list[2], TOKENS, EXPERTS, TOP, 1024)
    route_weight = jnp.clip(jnp.exp(math.log(1.0) - 2.9957323 * jax.random.uniform(key_list[3], (TOKENS, TOP), jnp.float32) ** steps_of(key_list[3], (TOKENS, TOP), ((0, 512),), -0.2, 0.2)), 0.05, 1.0)
    expert_slot = jax.random.permutation(key_list[4], EXPERTS).astype(jnp.int32)
    capacity = draw_capacity(jax.random.fold_in(key_list[7], 71), 0)
    gate_up = bell_draw(key_list[6], (EXPERTS, D, 2 * I), D ** -0.5, 0.125, ((0, 128), (1, 4)))
    return {"tokens": tokens, "cotangent": cotangent, "routes": routes, "route_weight": route_weight, "expert_slot": expert_slot, "capacity": capacity, "gate_up": gate_up}


def swiglu_grads(pre_act, cot_float, weight_rows, hidden_width):
    gate_part = pre_act[:, :hidden_width]
    up_part = pre_act[:, hidden_width:]
    sigmoid_gate = jax.nn.sigmoid(gate_part)
    active = gate_part * sigmoid_gate
    hidden = active * up_part
    scaled = weight_rows[:, None] * cot_float
    grad_up = scaled * active
    grad_gate = scaled * up_part * sigmoid_gate * (1.0 + gate_part * (1.0 - sigmoid_gate))
    packed = jnp.concatenate([grad_gate, grad_up], axis=1).astype(jnp.bfloat16)
    return packed, jnp.sum(hidden * cot_float, axis=1)


def reference(tokens, cotangent, routes, route_weight, expert_slot, capacity, gate_up):
    block_rows = TOK_DEV * TOP
    total_routes = TOKENS * TOP
    flat_routes = routes.reshape(-1).astype(jnp.int32)
    expert_ids = jnp.arange(EXPERTS, dtype=jnp.int32)
    blocked = flat_routes.reshape(-1, block_rows)
    onehot = (blocked[:, :, None] == expert_ids[None, None, :]).astype(jnp.int32)
    earlier = (jnp.cumsum(onehot, axis=1) - onehot).astype(jnp.int32)
    route_rank = jnp.sum(earlier * onehot, axis=2).astype(jnp.int32).reshape(-1)
    route_slot = expert_slot[flat_routes].astype(jnp.int32)
    is_kept = route_rank < capacity[route_slot]
    route_ids = jnp.arange(total_routes, dtype=jnp.int32)
    block_ids = route_ids // block_rows
    source_ids = block_ids // N_DP
    replica_ids = block_ids % N_DP
    per_slot = N_DP * N_EXPERT * CAP
    position = ((route_slot * N_DP + replica_ids) * N_EXPERT + source_ids) * CAP + route_rank
    position = jnp.where(is_kept, position, EXPERTS * per_slot).astype(jnp.int32)
    table = jnp.full((EXPERTS * per_slot,), total_routes, jnp.int32)
    table = table.at[position].set(route_ids, mode="drop").reshape(EXPERTS, per_slot)
    tokens_pad = jnp.concatenate([tokens, jnp.zeros((1, D), jnp.bfloat16)], axis=0)
    cot_pad = jnp.concatenate([cotangent.reshape(total_routes, I), jnp.zeros((1, I), jnp.bfloat16)], axis=0)
    weight_pad = jnp.concatenate([route_weight.reshape(-1), jnp.zeros((1,), jnp.float32)], axis=0)

    def per_expert(carry, inputs):
        input_acc, router_acc = carry
        row_ids, weight = inputs
        token_ids = (row_ids // TOP).astype(jnp.int32)
        rows_in = tokens_pad[token_ids]
        cot_float = cot_pad[row_ids].astype(jnp.float32)
        weight_rows = weight_pad[row_ids]
        pre_act = jnp.dot(rows_in, weight, preferred_element_type=jnp.float32)
        row_grad, router_rows = swiglu_grads(pre_act, cot_float, weight_rows, I)
        input_rows = jnp.dot(row_grad, weight.T, preferred_element_type=jnp.float32).astype(jnp.bfloat16)
        input_acc = input_acc.at[token_ids].add(input_rows.astype(jnp.float32))
        router_acc = router_acc.at[row_ids].add(router_rows)
        rows_four = rows_in.astype(jnp.float32).reshape(N_DP, N_EXPERT, CAP, D)
        grads_four = row_grad.astype(jnp.float32).reshape(N_DP, N_EXPERT, CAP, 2 * I)
        even_part = jnp.einsum("qskd,qskf->qdf", rows_four[:, :, 0::2], grads_four[:, :, 0::2]).astype(jnp.bfloat16)
        odd_part = jnp.einsum("qskd,qskf->qdf", rows_four[:, :, 1::2], grads_four[:, :, 1::2]).astype(jnp.bfloat16)
        pair_sum = (even_part.astype(jnp.float32) + odd_part.astype(jnp.float32)).astype(jnp.bfloat16)
        expert_grad = jnp.sum(pair_sum.astype(jnp.float32), axis=0).astype(jnp.bfloat16)
        return (input_acc, router_acc), expert_grad

    start = (jnp.zeros((TOKENS + 1, D), jnp.float32), jnp.zeros((total_routes + 1,), jnp.float32))
    (input_acc, router_acc), gate_up_grad = lax.scan(per_expert, start, (table, gate_up))
    token_grad = input_acc[:TOKENS].astype(jnp.bfloat16)
    route_weight_grad = router_acc[:total_routes].reshape(TOKENS, TOP)
    return (token_grad, route_weight_grad, gate_up_grad)
```

```python
import jax
import jax.numpy as jnp
from jax import lax
from jax.experimental import pallas as pl
from jax.experimental.pallas import tpu as pltpu
from jax.sharding import PartitionSpec as P

BF = jnp.bfloat16
F32 = jnp.float32
VMEM_BYTES = 48 * 1024 * 1024
TAIL = 128


def params():
    return pltpu.CompilerParams(vmem_limit_bytes=VMEM_BYTES)


def whole():
    return pl.BlockSpec(memory_space=pltpu.VMEM)


def scalars():
    return pl.BlockSpec(memory_space=pltpu.SMEM)


def iota(shape, dim):
    return lax.broadcasted_iota(jnp.int32, shape, dim)


def mm(a, b, ca=1, cb=0):
    return lax.dot_general(a, b, (((ca,), (cb,)), ((), ())), preferred_element_type=F32)


def token_of_route(routes, tokens, top):
    return ((iota((routes, tokens), 0) // top) == iota((routes, tokens), 1)).astype(BF)


def gather_rows(target, weight, tokens, cot, top, out_ref):
    rows = out_ref.shape[0]
    routes = target.shape[1]
    width = tokens.shape[1]
    hit = iota((rows, routes), 0) == target
    by_token = mm(hit.astype(BF), token_of_route(routes, tokens.shape[0], top)).astype(BF)
    out_ref[:, :width] = mm(by_token, tokens[...]).astype(BF)
    out_ref[:, width:] = mm(jnp.where(hit, weight, 0.0).astype(BF), cot[...]).astype(BF)


def pack_first(routes_ref, weight_ref, slot_ref, cap_ref, tokens_ref, cot_ref, out_ref, target_ref):
    experts = slot_ref.shape[1]
    routes = routes_ref.shape[1]
    tokens = tokens_ref.shape[0]
    top = routes // tokens
    named = iota((experts, routes), 0) == routes_ref[...]
    owner = token_of_route(routes, tokens, top)
    chosen = mm(named.astype(BF), owner)
    before = (iota((tokens, tokens), 0) < iota((tokens, tokens), 1)).astype(BF)
    earlier = mm(mm(chosen.astype(BF), before).astype(BF), owner, 1, 1)
    rank = jnp.sum(jnp.where(named, earlier, 0.0), axis=0, keepdims=True).astype(jnp.int32)
    square = (experts, experts)
    slot_col = jnp.sum(
        jnp.where(iota(square, 0) == iota(square, 1), slot_ref[...], 0), axis=1, keepdims=True
    )
    cap_col = jnp.sum(
        jnp.where(iota(square, 1) == slot_col, cap_ref[...], 0), axis=1, keepdims=True
    )
    slot = jnp.sum(jnp.where(named, slot_col, 0), axis=0, keepdims=True)
    cap = jnp.sum(jnp.where(named, cap_col, 0), axis=0, keepdims=True)
    kept = rank < cap
    far = rank >= 4
    place = jnp.where(far, 7 - rank, rank)
    half = experts // 2
    dest = jnp.where(far, jnp.where(slot >= half, slot - half, slot + half), slot)
    outer = jnp.where(kept & (place >= 2), dest * 2 + place - 2, -1)
    inner = jnp.where(kept & (place < 2), dest * 2 + place, -1)
    target_ref[0:1, :] = outer
    target_ref[1:2, :] = inner
    gather_rows(outer, weight_ref[...], tokens_ref, cot_ref, top, out_ref)


def pack_second(target_ref, weight_ref, tokens_ref, cot_ref, out_ref):
    top = target_ref.shape[1] // tokens_ref.shape[0]
    gather_rows(target_ref[1:2, :], weight_ref[...], tokens_ref, cot_ref, top, out_ref)


def serve(rows_ref, valid, weights_ref):
    width = weights_ref.shape[0]
    hidden = weights_ref.shape[1] // 2
    pre = mm(rows_ref[:, :width], weights_ref[...])
    scaled = rows_ref[:, width:].astype(F32)
    if valid is not None:
        scaled = jnp.where(valid, scaled, 0.0)
    gate = pre[:, :hidden]
    up = pre[:, hidden:]
    sig = jax.nn.sigmoid(gate)
    active = gate * sig
    grad_up = scaled * active
    grad_gate = scaled * up * sig * (1.0 + gate * (1.0 - sig))
    grad = jnp.concatenate([grad_gate, grad_up], axis=1).astype(BF)
    router = jnp.sum(grad_up * up, axis=1, keepdims=True)
    back = mm(grad, weights_ref[...], 1, 1).astype(BF)
    return grad, router, back


def split_router(router, lane):
    high = router.astype(BF).astype(F32)
    low = router - high
    lanes = iota((router.shape[0], TAIL), 1)
    return jnp.where(lanes == lane, high, jnp.where(lanes == lane + 1, low, 0.0))


def serve_outer(cap_ref, own_ref, far_ref, weights_ref, own_back, far_back, own_grad, far_grad):
    width = weights_ref.shape[0]
    cap = cap_ref[0]
    grad, router, back = serve(far_ref, cap > 4, weights_ref)
    far_grad[...] = grad
    far_back[:, :width] = back
    far_back[:, width:] = split_router(router, 0).astype(BF)
    grad, router, back = serve(own_ref, cap > 2, weights_ref)
    own_grad[...] = grad
    own_back[:, :width] = back
    own_back[:, width:] = split_router(router, 0).astype(BF)


def serve_inner(rows_ref, weights_ref, own_back, swapped_back, out_ref, grad_ref):
    width = weights_ref.shape[0]
    grad, router, back = serve(rows_ref, None, weights_ref)
    grad_ref[...] = grad
    out_ref[:, :width] = own_back[:, :width] + swapped_back[:, :width]
    out_ref[:, width : 2 * width] = back
    out_ref[:, 2 * width :] = (
        own_back[:, width:].astype(F32)
        + swapped_back[:, width:].astype(F32)
        + split_router(router, 2)
    ).astype(BF)


def weight_grad(rows_a, rows_b, rows_c, grad_a, grad_b, grad_c, out_ref):
    total = mm(rows_a[...], grad_a[...], 0, 0)
    total += mm(rows_b[...], grad_b[...], 0, 0)
    total += mm(rows_c[...], grad_c[...], 0, 0)
    out_ref[...] = total.astype(BF)


def unpack(target_ref, weight_ref, back_ref, token_ref, router_ref):
    tokens, width = token_ref.shape
    routes = target_ref.shape[1]
    rows = back_ref.shape[0]
    owner = token_of_route(routes, tokens, routes // tokens)
    total = None
    router = None
    for part in range(2):
        hit = (iota((rows, routes), 0) == target_ref[part : part + 1, :]).astype(BF)
        by_token = mm(owner, hit, 0, 1).astype(BF)
        term = mm(by_token, back_ref[:, part * width : (part + 1) * width])
        total = term if total is None else total + term
        found = mm(back_ref[:, 2 * width :], hit, 0, 0)
        value = found[2 * part : 2 * part + 1, :] + found[2 * part + 1 : 2 * part + 2, :]
        router = value if router is None else router + value
    token_ref[...] = total.astype(BF)
    router_ref[...] = router / weight_ref[...].astype(BF).astype(F32)


def call(kernel, out, specs, flops, moved, *args):
    return pl.pallas_call(
        kernel,
        out_shape=[jax.ShapeDtypeStruct(s, d) for s, d in out],
        in_specs=specs,
        out_specs=[whole() for _ in out],
        compiler_params=params(),
        cost_estimate=pl.CostEstimate(flops=flops, bytes_accessed=moved, transcendentals=0),
    )(*args)


def exchange(value, count):
    one = value.reshape(count, -1, value.shape[-1])
    return lax.all_to_all(one, "expert", split_axis=0, concat_axis=0, tiled=True).reshape(
        value.shape
    )


def local(tokens, cotangent, routes, route_weight, expert_slot, capacity, gate_up):
    count = lax.axis_size("expert")
    token_rows, width = tokens.shape
    top = routes.shape[1]
    hidden = cotangent.shape[2]
    n_routes = token_rows * top
    rows = 2 * count
    route_row = routes.reshape(1, n_routes)
    weight_row = route_weight.reshape(1, n_routes)
    cot = cotangent.reshape(n_routes, hidden)
    my_cap = lax.dynamic_slice(capacity, (lax.axis_index("expert"),), (1,))
    swap = [(s, (s + count // 2) % count) for s in range(count)]

    weights = lax.all_gather(gate_up, "dp", axis=1, tiled=True)[0]
    pack_flops = 2 * rows * n_routes * (hidden + 2 * token_rows)
    row_shape = ((rows, width + hidden), BF)
    send_outer, target = call(
        pack_first,
        [row_shape, ((2, n_routes), jnp.int32)],
        [whole()] * 6,
        pack_flops,
        3 << 20,
        route_row,
        weight_row,
        expert_slot.reshape(1, count),
        capacity.reshape(1, count),
        tokens,
        cot,
    )
    recv_outer = exchange(send_outer, count)
    (send_inner,) = call(
        pack_second, [row_shape], [whole()] * 4, pack_flops, 3 << 20, target, weight_row, tokens, cot
    )
    recv_inner = exchange(send_inner, count)
    far_outer = lax.ppermute(recv_outer, "expert", swap)
    serve_flops = 2 * rows * width * 4 * hidden
    back_shape = ((rows, width + TAIL), BF)
    grad_shape = ((rows, 2 * hidden), BF)
    own_back, far_back, own_grad, far_grad = call(
        serve_outer,
        [back_shape, back_shape, grad_shape, grad_shape],
        [scalars()] + [whole()] * 3,
        2 * serve_flops,
        8 << 20,
        my_cap,
        recv_outer,
        far_outer,
        weights,
    )
    swapped_back = lax.ppermute(far_back, "expert", swap)
    send_back, inner_grad = call(
        serve_inner,
        [((rows, 2 * width + TAIL), BF), grad_shape],
        [whole()] * 4,
        serve_flops,
        8 << 20,
        recv_inner,
        weights,
        own_back,
        swapped_back,
    )
    back = exchange(send_back, count)

    block = 512
    row_spec = pl.BlockSpec((rows, block), lambda i: (0, i))
    grad_spec = pl.BlockSpec((rows, 2 * hidden), lambda i: (0, 0))
    part = pl.pallas_call(
        weight_grad,
        grid=(width // block,),
        out_shape=jax.ShapeDtypeStruct((width, 2 * hidden), BF),
        in_specs=[row_spec] * 3 + [grad_spec] * 3,
        out_specs=pl.BlockSpec((block, 2 * hidden), lambda i: (i, 0)),
        compiler_params=params(),
        cost_estimate=pl.CostEstimate(
            flops=6 * rows * width * 2 * hidden, bytes_accessed=8 << 20, transcendentals=0
        ),
    )(recv_outer, far_outer, recv_inner, own_grad, far_grad, inner_grad)
    gate_up_grad = lax.psum_scatter(part, "dp", scatter_dimension=0, tiled=True)[None]

    token_grad, router = call(
        unpack,
        [((token_rows, width), BF), ((1, n_routes), F32)],
        [whole()] * 3,
        4 * rows * n_routes * 2 * token_rows,
        4 << 20,
        target,
        weight_row,
        back,
    )
    return token_grad, router.reshape(token_rows, top), gate_up_grad


def solution(mesh):
    in_specs = (
        P(("expert", "dp"), None),
        P(("expert", "dp"), None, None),
        P(("expert", "dp"), None),
        P(("expert", "dp"), None),
        P(),
        P(),
        P("expert", "dp", None),
    )
    out_specs = (P(("expert", "dp"), None), P(("expert", "dp"), None), P("expert", "dp", None))
    return jax.shard_map(local, mesh=mesh, in_specs=in_specs, out_specs=out_specs, check_vma=False)
```

```python
import jax
import jax.numpy as jnp
from jax import lax
from jax.experimental import pallas as pl
from jax.experimental.pallas import tpu as pltpu
from jax.sharding import PartitionSpec as P

BF = jnp.bfloat16
F32 = jnp.float32
VMEM_BYTES = 48 * 1024 * 1024
TAIL = 128


def params():
    return pltpu.CompilerParams(vmem_limit_bytes=VMEM_BYTES)


def whole():
    return pl.BlockSpec(memory_space=pltpu.VMEM)


def scalars():
    return pl.BlockSpec(memory_space=pltpu.SMEM)


def iota(shape, dim):
    return lax.broadcasted_iota(jnp.int32, shape, dim)


def mm(a, b, ca=1, cb=0):
    return lax.dot_general(a, b, (((ca,), (cb,)), ((), ())), preferred_element_type=F32)


def token_of_route(routes, tokens, top):
    return ((iota((routes, tokens), 0) // top) == iota((routes, tokens), 1)).astype(BF)


def gather_rows(target, weight, tokens, cot, top, out_ref, start):
    rows = out_ref.shape[0]
    routes = target.shape[1]
    width = tokens.shape[1]
    hidden = cot.shape[1]
    hit = iota((rows, routes), 0) == target
    by_token = mm(hit.astype(BF), token_of_route(routes, tokens.shape[0], top)).astype(BF)
    out_ref[:, start : start + width] = mm(by_token, tokens[...]).astype(BF)
    out_ref[:, start + width : start + width + hidden] = mm(
        jnp.where(hit, weight, 0.0).astype(BF), cot[...]
    ).astype(BF)


def pack(routes_ref, weight_ref, slot_ref, cap_ref, tokens_ref, cot_ref, out_ref, target_ref):
    experts = slot_ref.shape[1]
    routes = routes_ref.shape[1]
    tokens = tokens_ref.shape[0]
    top = routes // tokens
    named = iota((experts, routes), 0) == routes_ref[...]
    owner = token_of_route(routes, tokens, top)
    chosen = mm(named.astype(BF), owner)
    before = (iota((tokens, tokens), 0) < iota((tokens, tokens), 1)).astype(BF)
    earlier = mm(mm(chosen.astype(BF), before).astype(BF), owner, 1, 1)
    rank = jnp.sum(jnp.where(named, earlier, 0.0), axis=0, keepdims=True).astype(jnp.int32)
    square = (experts, experts)
    slot_col = jnp.sum(
        jnp.where(iota(square, 0) == iota(square, 1), slot_ref[...], 0), axis=1, keepdims=True
    )
    cap_col = jnp.sum(
        jnp.where(iota(square, 1) == slot_col, cap_ref[...], 0), axis=1, keepdims=True
    )
    slot = jnp.sum(jnp.where(named, slot_col, 0), axis=0, keepdims=True)
    cap = jnp.sum(jnp.where(named, cap_col, 0), axis=0, keepdims=True)
    kept = rank < cap
    far = rank >= 4
    place = jnp.where(far, 7 - rank, rank)
    half = experts // 2
    dest = jnp.where(far, jnp.where(slot >= half, slot - half, slot + half), slot)
    outer = jnp.where(kept & (place >= 2), dest * 2 + place - 2, -1)
    inner = jnp.where(kept & (place < 2), dest * 2 + place, -1)
    target_ref[0:1, :] = inner
    target_ref[1:2, :] = outer
    part = tokens_ref.shape[1] + cot_ref.shape[1]
    gather_rows(inner, weight_ref[...], tokens_ref, cot_ref, top, out_ref, 0)
    gather_rows(outer, weight_ref[...], tokens_ref, cot_ref, top, out_ref, part)


def serve(rows_ref, start, weights_ref):
    width = weights_ref.shape[0]
    hidden = weights_ref.shape[1] // 2
    pre = mm(rows_ref[:, start : start + width], weights_ref[...])
    scaled = rows_ref[:, start + width : start + width + hidden].astype(F32)
    gate = pre[:, :hidden]
    up = pre[:, hidden:]
    sig = jax.nn.sigmoid(gate)
    active = gate * sig
    grad_up = scaled * active
    grad_gate = scaled * up * sig * (1.0 + gate * (1.0 - sig))
    grad = jnp.concatenate([grad_gate, grad_up], axis=1).astype(BF)
    router = jnp.sum(grad_up * up, axis=1, keepdims=True)
    back = mm(grad, weights_ref[...], 1, 1).astype(BF)
    return grad, router, back


def split_router(router, lane):
    high = router.astype(BF).astype(F32)
    low = router - high
    lanes = iota((router.shape[0], TAIL), 1)
    return jnp.where(lanes == lane, high, jnp.where(lanes == lane + 1, low, 0.0))


def serve_all(cap_ref, rows_ref, own_ref, partner_ref, out_ref, inner_ref, outer_ref, far_ref):
    width = own_ref.shape[0]
    part = rows_ref.shape[1] // 2
    grad, router, back = serve(rows_ref, 0, own_ref)
    inner_ref[...] = grad
    out_ref[:, :width] = back
    tail = split_router(router, 0)

    def outer_with(weights_ref, mine_ref, other_ref):
        grad, router, back = serve(rows_ref, part, weights_ref)
        mine_ref[...] = grad
        other_ref[...] = jnp.zeros_like(grad)
        out_ref[:, width : 2 * width] = back
        out_ref[:, 2 * width :] = (tail + split_router(router, 2)).astype(BF)

    is_own = cap_ref[0] > 2

    @pl.when(is_own)
    def _():
        outer_with(own_ref, outer_ref, far_ref)

    @pl.when(jnp.logical_not(is_own))
    def _():
        outer_with(partner_ref, far_ref, outer_ref)


def weight_grads(inner_rows, outer_rows, inner_grad, outer_grad, far_grad, own_ref, far_ref):
    total = mm(inner_rows[...], inner_grad[...], 0, 0)
    total += mm(outer_rows[...], outer_grad[...], 0, 0)
    own_ref[...] = total.astype(BF)
    far_ref[...] = mm(outer_rows[...], far_grad[...], 0, 0).astype(BF)


def unpack(target_ref, weight_ref, back_ref, token_ref, router_ref):
    tokens, width = token_ref.shape
    routes = target_ref.shape[1]
    rows = back_ref.shape[0]
    owner = token_of_route(routes, tokens, routes // tokens)
    total = None
    router = None
    for part in range(2):
        hit = (iota((rows, routes), 0) == target_ref[part : part + 1, :]).astype(BF)
        by_token = mm(owner, hit, 0, 1).astype(BF)
        term = mm(by_token, back_ref[:, part * width : (part + 1) * width])
        total = term if total is None else total + term
        found = mm(back_ref[:, 2 * width :], hit, 0, 0)
        value = found[2 * part : 2 * part + 1, :] + found[2 * part + 1 : 2 * part + 2, :]
        router = value if router is None else router + value
    token_ref[...] = total.astype(BF)
    router_ref[...] = router / weight_ref[...].astype(BF).astype(F32)


def call(kernel, out, specs, flops, moved, *args):
    return pl.pallas_call(
        kernel,
        out_shape=[jax.ShapeDtypeStruct(s, d) for s, d in out],
        in_specs=specs,
        out_specs=[whole() for _ in out],
        compiler_params=params(),
        cost_estimate=pl.CostEstimate(flops=flops, bytes_accessed=moved, transcendentals=0),
    )(*args)


def exchange(value, count):
    one = value.reshape(count, -1, value.shape[-1])
    return lax.all_to_all(one, "expert", split_axis=0, concat_axis=0, tiled=True).reshape(
        value.shape
    )


def local(tokens, cotangent, routes, route_weight, expert_slot, capacity, gate_up):
    count = lax.axis_size("expert")
    token_rows, width = tokens.shape
    top = routes.shape[1]
    hidden = cotangent.shape[2]
    n_routes = token_rows * top
    rows = 2 * count
    route_row = routes.reshape(1, n_routes)
    weight_row = route_weight.reshape(1, n_routes)
    cot = cotangent.reshape(n_routes, hidden)
    my_cap = lax.dynamic_slice(capacity, (lax.axis_index("expert"),), (1,))
    swap = [(s, (s + count // 2) % count) for s in range(count)]

    own_weights = lax.all_gather(gate_up, "dp", axis=1, tiled=True)[0]
    partner_shard = lax.ppermute(gate_up, "expert", swap)
    partner_weights = lax.all_gather(partner_shard, "dp", axis=1, tiled=True)[0]
    part = width + hidden
    send, target = call(
        pack,
        [((rows, 2 * part), BF), ((2, n_routes), jnp.int32)],
        [whole()] * 6,
        4 * rows * n_routes * (hidden + 2 * token_rows),
        4 << 20,
        route_row,
        weight_row,
        expert_slot.reshape(1, count),
        capacity.reshape(1, count),
        tokens,
        cot,
    )
    recv = exchange(send, count)
    grad_shape = ((rows, 2 * hidden), BF)
    send_back, inner_grad, outer_grad, far_grad = call(
        serve_all,
        [((rows, 2 * width + TAIL), BF), grad_shape, grad_shape, grad_shape],
        [scalars()] + [whole()] * 3,
        16 * rows * width * hidden,
        12 << 20,
        my_cap,
        recv,
        own_weights,
        partner_weights,
    )
    back = exchange(send_back, count)

    block = 128
    grad_spec = pl.BlockSpec((rows, 2 * hidden), lambda i: (0, 0))
    out_spec = pl.BlockSpec((block, 2 * hidden), lambda i: (i, 0))
    out = jax.ShapeDtypeStruct((width, 2 * hidden), BF)
    own_part, far_part = pl.pallas_call(
        weight_grads,
        grid=(width // block,),
        out_shape=[out, out],
        in_specs=[
            pl.BlockSpec((rows, block), lambda i: (0, i)),
            pl.BlockSpec((rows, block), lambda i: (0, i + part // block)),
            grad_spec,
            grad_spec,
            grad_spec,
        ],
        out_specs=[out_spec, out_spec],
        compiler_params=params(),
        cost_estimate=pl.CostEstimate(
            flops=12 * rows * width * hidden, bytes_accessed=10 << 20, transcendentals=0
        ),
    )(recv, recv, inner_grad, outer_grad, far_grad)
    far_shard = lax.psum_scatter(far_part, "dp", scatter_dimension=0, tiled=True)
    own_shard = lax.psum_scatter(own_part, "dp", scatter_dimension=0, tiled=True)
    moved_shard = lax.ppermute(far_shard, "expert", swap)
    gate_up_grad = (own_shard.astype(F32) + moved_shard.astype(F32)).astype(BF)[None]

    token_grad, router = call(
        unpack,
        [((token_rows, width), BF), ((1, n_routes), F32)],
        [whole()] * 3,
        4 * rows * n_routes * 2 * token_rows,
        4 << 20,
        target,
        weight_row,
        back,
    )
    return token_grad, router.reshape(token_rows, top), gate_up_grad


def solution(mesh):
    in_specs = (
        P(("expert", "dp"), None),
        P(("expert", "dp"), None, None),
        P(("expert", "dp"), None),
        P(("expert", "dp"), None),
        P(),
        P(),
        P("expert", "dp", None),
    )
    out_specs = (P(("expert", "dp"), None), P(("expert", "dp"), None), P("expert", "dp", None))
    return jax.shard_map(local, mesh=mesh, in_specs=in_specs, out_specs=out_specs, check_vma=False)
```

```python
import jax
import jax.numpy as jnp
from jax import lax
from jax.experimental import pallas as pl
from jax.experimental.pallas import tpu as pltpu
from jax.sharding import PartitionSpec as P

BF = jnp.bfloat16
F32 = jnp.float32
VMEM_BYTES = 40 * 1024 * 1024
VMEM_MOST = 56 * 1024 * 1024
TAIL = 128


def params(limit=VMEM_BYTES):
    return pltpu.CompilerParams(vmem_limit_bytes=limit)


def whole():
    return pl.BlockSpec(memory_space=pltpu.VMEM)


def in_hbm():
    return pl.BlockSpec(memory_space=pltpu.HBM)


def scalars():
    return pl.BlockSpec(memory_space=pltpu.SMEM)


def iota(shape, dim):
    return lax.broadcasted_iota(jnp.int32, shape, dim)


def mm(a, b, ca=1, cb=0):
    return lax.dot_general(a, b, (((ca,), (cb,)), ((), ())), preferred_element_type=F32)


def by_token_and_route(tokens, routes, top):
    shape = (tokens, routes)
    return (iota(shape, 0) == (iota(shape, 1) // top)).astype(BF)


def to_row(per_rank, owner, top):
    routes = owner.shape[1]
    spread = mm(per_rank.astype(F32).astype(BF), owner)
    mine = iota((top, routes), 0) == (iota((top, routes), 1) % top)
    return jnp.sum(jnp.where(mine, spread, 0.0), axis=0, keepdims=True)


def from_row(row, owner, top):
    routes = owner.shape[1]
    mine = iota((top, routes), 0) == (iota((top, routes), 1) % top)
    rest = jnp.where(mine, row, 0.0)
    total = None
    for _ in range(3):
        piece = rest.astype(BF)
        rest = rest - piece.astype(F32)
        term = mm(piece, owner, 1, 1)
        total = term if total is None else total + term
    return total


def copies(sems, *pairs):
    made = [pltpu.make_async_copy(src, dst, sems.at[i]) for i, (src, dst) in enumerate(pairs)]
    for one in made:
        one.start()
    return made


def route_targets(routes_row, owner, slot_row, cap_row):
    experts = slot_row.shape[1]
    tokens, routes = owner.shape
    named = iota((experts, routes), 0) == routes_row
    chosen = mm(named.astype(BF), owner, 1, 1)
    before = (iota((tokens, tokens), 0) < iota((tokens, tokens), 1)).astype(BF)
    earlier = mm(mm(chosen.astype(BF), before).astype(BF), owner)
    rank = jnp.sum(jnp.where(named, earlier, 0.0), axis=0, keepdims=True).astype(jnp.int32)
    square = (experts, experts)
    slot_col = jnp.sum(
        jnp.where(iota(square, 0) == iota(square, 1), slot_row, 0), axis=1, keepdims=True
    )
    cap_col = jnp.sum(jnp.where(iota(square, 1) == slot_col, cap_row, 0), axis=1, keepdims=True)
    slot = jnp.sum(jnp.where(named, slot_col, 0), axis=0, keepdims=True)
    cap = jnp.sum(jnp.where(named, cap_col, 0), axis=0, keepdims=True)
    kept = rank < cap
    far = rank >= 4
    place = jnp.where(far, 7 - rank, rank)
    half = experts // 2
    dest = jnp.where(far, jnp.where(slot >= half, slot - half, slot + half), slot)
    inner = jnp.where(kept & (place < 2), dest * 2 + place, -1)
    outer = jnp.where(kept & (place >= 2), dest * 2 + place - 2, -1)
    return inner, outer


def pack(
    routes_hbm, weight_hbm, slot_hbm, cap_hbm, tokens_hbm, cot_hbm, out_hbm, target_ref, scaled_ref,
    routes, weight, slot, cap, tokens, cot, out, sems, out_sems,
):
    top, n_tokens = routes.shape
    n_routes = top * n_tokens
    width = tokens.shape[1]
    hidden = cot.shape[1]
    part = width + hidden
    loads = copies(
        sems, (routes_hbm, routes), (slot_hbm, slot), (cap_hbm, cap), (weight_hbm, weight),
        (tokens_hbm, tokens), (cot_hbm, cot),
    )
    owner = by_token_and_route(n_tokens, n_routes, top)
    for one in loads[:4]:
        one.wait()
    routes_row = to_row(routes[...], owner, top).astype(jnp.int32)
    weight_row = to_row(weight[...], owner, top)
    scaled_ref[...] = weight_row
    targets = route_targets(routes_row, owner, slot[...], cap[...])
    target_ref[0:1, :] = targets[0]
    target_ref[1:2, :] = targets[1]
    rows = out.shape[0] * out.shape[1]
    loads[4].wait()
    stores = []
    for i, target in enumerate(targets):
        hit = iota((rows, n_routes), 0) == target
        pick = mm(hit.astype(BF), owner, 1, 1).astype(BF)
        start = i * part
        moved = mm(pick, tokens[...]).astype(BF)
        out[:, :, start : start + width] = moved.reshape(rows // 2, 2, width)
        if i == 0:
            loads[5].wait()
        moved = mm(jnp.where(hit, weight_row, 0.0).astype(BF), cot[...]).astype(BF)
        out[:, :, start + width : start + part] = moved.reshape(rows // 2, 2, hidden)
        span = pl.ds(start, part)
        store = pltpu.make_async_copy(out.at[:, :, span], out_hbm.at[:, :, span], out_sems.at[i])
        store.start()
        stores.append(store)
    for one in stores:
        one.wait()


def split_router(router, lane):
    high = router.astype(BF).astype(F32)
    low = router - high
    lanes = iota((router.shape[0], TAIL), 1)
    return jnp.where(lanes == lane, high, jnp.where(lanes == lane + 1, low, 0.0))


def serve(rows, scaled, weights):
    hidden = weights.shape[1] // 2
    pre = mm(rows, weights[...])
    scaled = scaled.astype(F32)
    gate = pre[:, :hidden]
    up = pre[:, hidden:]
    sig = jax.nn.sigmoid(gate)
    active = gate * sig
    grad_up = scaled * active
    grad_gate = scaled * up * sig * (1.0 + gate * (1.0 - sig))
    grad = jnp.concatenate([grad_gate, grad_up], axis=1).astype(BF)
    router = jnp.sum(grad_up * up, axis=1, keepdims=True)
    back = mm(grad, weights[...], 1, 1).astype(BF)
    return grad, router, back


def serve_all(
    cap_ref, recv_hbm, own_hbm, partner_hbm, back_hbm, rows_hbm, grad_hbm,
    recv, own, other, back, all_rows, all_grads, sems, out_sems,
):
    width = own.shape[0]
    hidden = own.shape[1] // 2
    part = width + hidden
    sources = recv.shape[0]
    rows = 2 * sources
    chunks, _, chunk = all_rows.shape
    is_own = cap_ref[0] > 2
    spans = [pl.ds(0, part), pl.ds(part, part)]
    views = [(recv_hbm.at[:, :, s], recv.at[:, :, s]) for s in spans]
    loads = copies(sems, views[0], (own_hbm, own), views[1])

    @pl.when(is_own)
    def _():
        pltpu.make_async_copy(own_hbm, other, sems.at[3]).start()

    @pl.when(jnp.logical_not(is_own))
    def _():
        pltpu.make_async_copy(partner_hbm, other, sems.at[3]).start()

    stores = []

    def store(src, dst):
        one = pltpu.make_async_copy(src, dst, out_sems.at[len(stores)])
        one.start()
        stores.append(one)

    tail = None
    for i, weights in enumerate((own, other)):
        start = i * part
        span = pl.ds(i * rows, rows)
        loads[2 * i].wait()
        tokens = recv[:, :, start : start + width].reshape(rows, width)
        for c in range(chunks):
            all_rows[c, i * rows : (i + 1) * rows, :] = tokens[:, c * chunk : (c + 1) * chunk]
        store(all_rows.at[:, span, :], rows_hbm.at[:, span, :])
        scaled = recv[:, :, start + width : start + part].reshape(rows, hidden)
        if i == 0:
            loads[1].wait()
        else:
            pltpu.make_async_copy(own_hbm, other, sems.at[3]).wait()
        grad, router, result = serve(tokens, scaled, weights)
        all_grads[i * rows : (i + 1) * rows, :] = grad
        store(all_grads.at[span, :], grad_hbm.at[span, :])
        back[:, :, i * width : (i + 1) * width] = result.reshape(sources, 2, width)
        wide = width
        lanes = split_router(router, 2 * i)
        tail = lanes if tail is None else tail + lanes
        if i == 1:
            wide = width + TAIL
            back[:, :, 2 * width :] = tail.astype(BF).reshape(sources, 2, TAIL)
        out_span = pl.ds(i * width, wide)
        store(back.at[:, :, out_span], back_hbm.at[:, :, out_span])
    for one in stores:
        one.wait()


def weight_grads(cap_ref, me_ref, rows_0, rows_1, rows_2, rows_3, grads, own_ref, far_ref):
    received = (rows_0, rows_1, rows_2, rows_3)
    sources = len(received)
    half = rows_0.shape[0] // 2
    is_own = cap_ref[0] > 2
    inner = None
    outer = None
    for k, rows in enumerate(received):
        source = lax.rem(me_ref[0] + sources - k, sources)
        term = mm(rows[:half, :], grads[source, :half, :], 0, 0)
        inner = term if inner is None else inner + term
        term = mm(rows[half:, :], grads[source, half:, :], 0, 0)
        outer = term if outer is None else outer + term
    own_ref[...] = inner + jnp.where(is_own, outer, 0.0)
    far_ref[...] = jnp.where(is_own, 0.0, outer).astype(BF)


def unpack(target_ref, scaled_ref, back, token_ref, router_ref):
    n_tokens, width = token_ref.shape
    top = router_ref.shape[0]
    n_routes = top * n_tokens
    rows = 2 * back.shape[0]
    owner = by_token_and_route(n_tokens, n_routes, top)
    hits = [
        (iota((rows, n_routes), 0) == target_ref[i : i + 1, :]).astype(BF) for i in range(2)
    ]
    picks = [mm(owner, hit, 1, 1).astype(BF) for hit in hits]
    tail = back[:, :, 2 * width :].reshape(rows, TAIL)
    router = None
    for i, hit in enumerate(hits):
        found = mm(tail, hit, 0, 0)
        value = found[2 * i : 2 * i + 1, :] + found[2 * i + 1 : 2 * i + 2, :]
        router = value if router is None else router + value
    router_ref[...] = from_row(router / scaled_ref[...], owner, top)
    total = None
    for i, pick in enumerate(picks):
        term = mm(pick, back[:, :, i * width : (i + 1) * width].reshape(rows, width))
        total = term if total is None else total + term
    token_ref[...] = total.astype(BF)


def call(kernel, out, in_specs, out_specs, scratch, flops, moved, *args, limit=VMEM_BYTES):
    return pl.pallas_call(
        kernel,
        out_shape=[jax.ShapeDtypeStruct(s, d) for s, d in out],
        in_specs=in_specs,
        out_specs=out_specs,
        scratch_shapes=scratch,
        compiler_params=params(limit),
        cost_estimate=pl.CostEstimate(flops=flops, bytes_accessed=moved, transcendentals=0),
    )(*args)


def exchange(value):
    return lax.all_to_all(value, "expert", split_axis=0, concat_axis=0, tiled=True)


def local(tokens, cotangent, routes, route_weight, expert_slot, capacity, gate_up):
    count = lax.axis_size("expert")
    n_tokens, width = tokens.shape
    top = routes.shape[1]
    hidden = cotangent.shape[2]
    n_routes = n_tokens * top
    rows = 2 * count
    part = width + hidden
    my_cap = lax.dynamic_slice(capacity, (lax.axis_index("expert"),), (1,))
    swap = [(s, (s + count // 2) % count) for s in range(count)]
    dma = pltpu.SemaphoreType.DMA

    own_weights = lax.all_gather(gate_up, "dp", axis=1, tiled=True)[0]
    partner_shard = lax.ppermute(gate_up, "expert", swap)
    partner_weights = lax.all_gather(partner_shard, "dp", axis=1, tiled=True)[0]
    send, target, scaled = call(
        pack,
        [((count, 2, 2 * part), BF), ((2, n_routes), jnp.int32), ((1, n_routes), F32)],
        [in_hbm()] * 6,
        [in_hbm(), whole(), whole()],
        [
            pltpu.VMEM((top, n_tokens), jnp.int32),
            pltpu.VMEM((top, n_tokens), F32),
            pltpu.VMEM((1, count), jnp.int32),
            pltpu.VMEM((1, count), jnp.int32),
            pltpu.VMEM((n_tokens, width), BF),
            pltpu.VMEM((n_routes, hidden), BF),
            pltpu.VMEM((count, 2, 2 * part), BF),
            dma((6,)),
            dma((2,)),
        ],
        4 * rows * n_routes * (hidden + 2 * n_tokens),
        4 << 20,
        routes.T,
        route_weight.T,
        expert_slot.reshape(1, count),
        capacity.reshape(1, count),
        tokens,
        cotangent.reshape(n_routes, hidden),
        limit=VMEM_MOST,
    )
    recv = exchange(send)
    replicas = lax.axis_size("dp")
    chunk = width // replicas
    send_back, sent_rows, grads = call(
        serve_all,
        [
            ((count, 2, 2 * width + TAIL), BF),
            ((replicas, 2 * rows, chunk), BF),
            ((2 * rows, 2 * hidden), BF),
        ],
        [scalars()] + [in_hbm()] * 3,
        [in_hbm()] * 3,
        [
            pltpu.VMEM((count, 2, 2 * part), BF),
            pltpu.VMEM((width, 2 * hidden), BF),
            pltpu.VMEM((width, 2 * hidden), BF),
            pltpu.VMEM((count, 2, 2 * width + TAIL), BF),
            pltpu.VMEM((replicas, 2 * rows, chunk), BF),
            pltpu.VMEM((2 * rows, 2 * hidden), BF),
            dma((4,)),
            dma((6,)),
        ],
        16 * rows * width * hidden,
        12 << 20,
        my_cap,
        recv,
        own_weights,
        partner_weights,
        limit=VMEM_MOST,
    )
    back = exchange(send_back)
    all_grads = lax.all_gather(grads, "dp", axis=0, tiled=False)
    me = lax.axis_index("dp")
    received = []
    for k in range(replicas):
        piece = lax.dynamic_index_in_dim(
            sent_rows, lax.rem(me + k, replicas), axis=0, keepdims=False
        )
        if k:
            piece = lax.ppermute(piece, "dp", [(q, (q + k) % replicas) for q in range(replicas)])
        received.append(piece)
    shard = (chunk, 2 * hidden)
    own_shard, far_shard = call(
        weight_grads,
        [(shard, F32), (shard, BF)],
        [scalars(), scalars()] + [whole()] * 5,
        [whole()] * 2,
        [],
        8 * replicas * rows * chunk * hidden,
        8 << 20,
        my_cap,
        me.reshape(1),
        *received,
        all_grads,
    )
    moved_shard = lax.ppermute(far_shard, "expert", swap)
    gate_up_grad = (own_shard + moved_shard.astype(F32)).astype(BF)[None]

    token_grad, router = call(
        unpack,
        [((n_tokens, width), BF), ((top, n_tokens), F32)],
        [whole()] * 3,
        [whole()] * 2,
        [],
        4 * rows * n_routes * 2 * n_tokens,
        4 << 20,
        target,
        scaled,
        back,
    )
    return token_grad, router.T, gate_up_grad


def solution(mesh):
    in_specs = (
        P(("expert", "dp"), None),
        P(("expert", "dp"), None, None),
        P(("expert", "dp"), None),
        P(("expert", "dp"), None),
        P(),
        P(),
        P("expert", "dp", None),
    )
    out_specs = (P(("expert", "dp"), None), P(("expert", "dp"), None), P("expert", "dp", None))
    return jax.shard_map(local, mesh=mesh, in_specs=in_specs, out_specs=out_specs, check_vma=False)
```

```python
import jax
import jax.numpy as jnp
from jax import lax
from jax.experimental import pallas as pl
from jax.experimental.pallas import tpu as pltpu
from jax.sharding import PartitionSpec as P

BF = jnp.bfloat16
F32 = jnp.float32
VMEM_BYTES = 40 * 1024 * 1024
VMEM_MOST = 56 * 1024 * 1024
TAIL = 128
PIECES = 4
VMEM_SERVE = 47 * 1024 * 1024


def params(limit=VMEM_BYTES):
    return pltpu.CompilerParams(vmem_limit_bytes=limit)


def whole():
    return pl.BlockSpec(memory_space=pltpu.VMEM)


def in_hbm():
    return pl.BlockSpec(memory_space=pltpu.HBM)


def scalars():
    return pl.BlockSpec(memory_space=pltpu.SMEM)


def iota(shape, dim):
    return lax.broadcasted_iota(jnp.int32, shape, dim)


def mm(a, b, ca=1, cb=0):
    return lax.dot_general(a, b, (((ca,), (cb,)), ((), ())), preferred_element_type=F32)


def by_token_and_route(tokens, routes, top):
    shape = (tokens, routes)
    return (iota(shape, 0) == (iota(shape, 1) // top)).astype(BF)


def to_row(per_rank, owner, top):
    routes = owner.shape[1]
    spread = mm(per_rank.astype(F32).astype(BF), owner)
    mine = iota((top, routes), 0) == (iota((top, routes), 1) % top)
    return jnp.sum(jnp.where(mine, spread, 0.0), axis=0, keepdims=True)


def from_row(row, owner, top):
    routes = owner.shape[1]
    mine = iota((top, routes), 0) == (iota((top, routes), 1) % top)
    rest = jnp.where(mine, row, 0.0)
    total = None
    for _ in range(3):
        piece = rest.astype(BF)
        rest = rest - piece.astype(F32)
        term = mm(piece, owner, 1, 1)
        total = term if total is None else total + term
    return total


def copies(sems, *pairs):
    made = [pltpu.make_async_copy(src, dst, sems.at[i]) for i, (src, dst) in enumerate(pairs)]
    for one in made:
        one.start()
    return made


def route_targets(routes_row, owner, slot_row, cap_row):
    experts = slot_row.shape[1]
    tokens, routes = owner.shape
    named = iota((experts, routes), 0) == routes_row
    chosen = mm(named.astype(BF), owner, 1, 1)
    before = (iota((tokens, tokens), 0) < iota((tokens, tokens), 1)).astype(BF)
    earlier = mm(mm(chosen.astype(BF), before).astype(BF), owner)
    rank = jnp.sum(jnp.where(named, earlier, 0.0), axis=0, keepdims=True).astype(jnp.int32)
    square = (experts, experts)
    slot_col = jnp.sum(
        jnp.where(iota(square, 0) == iota(square, 1), slot_row, 0), axis=1, keepdims=True
    )
    cap_col = jnp.sum(jnp.where(iota(square, 1) == slot_col, cap_row, 0), axis=1, keepdims=True)
    slot = jnp.sum(jnp.where(named, slot_col, 0), axis=0, keepdims=True)
    cap = jnp.sum(jnp.where(named, cap_col, 0), axis=0, keepdims=True)
    kept = rank < cap
    far = rank >= 4
    place = jnp.where(far, 7 - rank, rank)
    half = experts // 2
    dest = jnp.where(far, jnp.where(slot >= half, slot - half, slot + half), slot)
    inner = jnp.where(kept & (place < 2), dest * 2 + place, -1)
    outer = jnp.where(kept & (place >= 2), dest * 2 + place - 2, -1)
    return inner, outer


def pack(
    routes_hbm, weight_hbm, slot_hbm, cap_hbm, tokens_hbm, cot_hbm, out_hbm, target_ref, scaled_ref,
    routes, weight, slot, cap, tokens, cot, out, sems, out_sems,
):
    top, n_tokens = routes.shape
    n_routes = top * n_tokens
    width = tokens.shape[1]
    hidden = cot.shape[1]
    part = width + hidden
    loads = copies(
        sems, (routes_hbm, routes), (slot_hbm, slot), (cap_hbm, cap), (weight_hbm, weight),
        (tokens_hbm, tokens), (cot_hbm, cot),
    )
    owner = by_token_and_route(n_tokens, n_routes, top)
    for one in loads[:4]:
        one.wait()
    routes_row = to_row(routes[...], owner, top).astype(jnp.int32)
    weight_row = to_row(weight[...], owner, top)
    scaled_ref[...] = weight_row
    targets = route_targets(routes_row, owner, slot[...], cap[...])
    target_ref[0:1, :] = targets[0]
    target_ref[1:2, :] = targets[1]
    rows = out.shape[0] * out.shape[1]
    loads[4].wait()
    stores = []
    for i, target in enumerate(targets):
        hit = iota((rows, n_routes), 0) == target
        pick = mm(hit.astype(BF), owner, 1, 1).astype(BF)
        start = i * part
        moved = mm(pick, tokens[...]).astype(BF)
        out[:, :, start : start + width] = moved.reshape(rows // 2, 2, width)
        if i == 0:
            loads[5].wait()
        moved = mm(jnp.where(hit, weight_row, 0.0).astype(BF), cot[...]).astype(BF)
        out[:, :, start + width : start + part] = moved.reshape(rows // 2, 2, hidden)
        span = pl.ds(start, part)
        store = pltpu.make_async_copy(out.at[:, :, span], out_hbm.at[:, :, span], out_sems.at[i])
        store.start()
        stores.append(store)
    for one in stores:
        one.wait()


def split_router(router, lane):
    high = router.astype(BF).astype(F32)
    low = router - high
    lanes = iota((router.shape[0], TAIL), 1)
    return jnp.where(lanes == lane, high, jnp.where(lanes == lane + 1, low, 0.0))


def serve(rows, scaled, weights, loads):
    width, hidden = weights.shape[0], weights.shape[1] // 2
    pre = None
    deep = width // len(loads)
    for k, load in enumerate(loads):
        load.wait()
        span = slice(k * deep, (k + 1) * deep)
        term = mm(rows[:, span], weights[span, :])
        pre = term if pre is None else pre + term
    scaled = scaled.astype(F32)
    gate = pre[:, :hidden]
    up = pre[:, hidden:]
    sig = jax.nn.sigmoid(gate)
    active = gate * sig
    grad_up = scaled * active
    grad_gate = scaled * up * sig * (1.0 + gate * (1.0 - sig))
    grad = jnp.concatenate([grad_gate, grad_up], axis=1).astype(BF)
    router = jnp.sum(grad_up * up, axis=1, keepdims=True)
    back = mm(grad, weights[...], 1, 1).astype(BF)
    return grad, router, back


def serve_all(
    cap_ref, recv, own_hbm, partner_hbm, back, grad_hbm, own, other, all_grads, sems, out_sems
):
    width = own.shape[0]
    hidden = own.shape[1] // 2
    part = width + hidden
    sources = recv.shape[0]
    rows = 2 * sources
    is_own = cap_ref[0] > 2
    deep = width // PIECES
    pieces = [pl.ds(k * deep, deep) for k in range(PIECES)]
    loads = copies(sems, *[(own_hbm.at[p], own.at[p]) for p in pieces])
    last = sems.at[PIECES]

    @pl.when(is_own)
    def _():
        pltpu.make_async_copy(own_hbm, other, last).start()

    @pl.when(jnp.logical_not(is_own))
    def _():
        pltpu.make_async_copy(partner_hbm, other, last).start()

    ready = (loads, [pltpu.make_async_copy(own_hbm, other, last)])
    stores = []
    tail = None
    for i, weights in enumerate((own, other)):
        start = i * part
        tokens = recv[:, :, start : start + width].reshape(rows, width)
        scaled = recv[:, :, start + width : start + part].reshape(rows, hidden)
        grad, router, result = serve(tokens, scaled, weights, ready[i])
        span = pl.ds(i * rows, rows)
        all_grads[i * rows : (i + 1) * rows, :] = grad
        store = pltpu.make_async_copy(all_grads.at[span], grad_hbm.at[span], out_sems.at[i])
        store.start()
        stores.append(store)
        back[:, :, i * width : (i + 1) * width] = result.reshape(sources, 2, width)
        lanes = split_router(router, 2 * i)
        tail = lanes if tail is None else tail + lanes
    back[:, :, 2 * width :] = tail.astype(BF).reshape(sources, 2, TAIL)
    for one in stores:
        one.wait()


def slice_rows(me_ref, recv, grads_hbm, *out_refs):
    del grads_hbm
    slices = len(out_refs)
    rows = 2 * recv.shape[0]
    part = recv.shape[2] // 2
    chunk = out_refs[0].shape[1]
    for k, out_ref in enumerate(out_refs):
        column = lax.rem(me_ref[0] + k, slices) * chunk
        for i in range(2):
            span = pl.ds(pl.multiple_of(i * part + column, 128), chunk)
            out_ref[i * rows : (i + 1) * rows, :] = recv[:, :, span].reshape(rows, chunk)


def weight_grads(cap_ref, me_ref, rows_0, rows_1, rows_2, rows_3, grads, own_ref, far_ref):
    received = (rows_0, rows_1, rows_2, rows_3)
    sources = len(received)
    half = rows_0.shape[0] // 2
    is_own = cap_ref[0] > 2
    inner = None
    outer = None
    for k, rows in enumerate(received):
        source = lax.rem(me_ref[0] + sources - k, sources)
        term = mm(rows[:half, :], grads[source, :half, :], 0, 0)
        inner = term if inner is None else inner + term
        term = mm(rows[half:, :], grads[source, half:, :], 0, 0)
        outer = term if outer is None else outer + term
    own_ref[...] = inner + jnp.where(is_own, outer, 0.0)
    far_ref[...] = jnp.where(is_own, 0.0, outer).astype(BF)


def unpack(target_ref, scaled_ref, back, token_ref, router_ref):
    n_tokens, width = token_ref.shape
    top = router_ref.shape[0]
    n_routes = top * n_tokens
    rows = 2 * back.shape[0]
    owner = by_token_and_route(n_tokens, n_routes, top)
    hits = [
        (iota((rows, n_routes), 0) == target_ref[i : i + 1, :]).astype(BF) for i in range(2)
    ]
    picks = [mm(owner, hit, 1, 1).astype(BF) for hit in hits]
    tail = back[:, :, 2 * width :].reshape(rows, TAIL)
    router = None
    for i, hit in enumerate(hits):
        found = mm(tail, hit, 0, 0)
        value = found[2 * i : 2 * i + 1, :] + found[2 * i + 1 : 2 * i + 2, :]
        router = value if router is None else router + value
    router_ref[...] = from_row(router / scaled_ref[...], owner, top)
    total = None
    for i, pick in enumerate(picks):
        term = mm(pick, back[:, :, i * width : (i + 1) * width].reshape(rows, width))
        total = term if total is None else total + term
    token_ref[...] = total.astype(BF)


def call(kernel, out, in_specs, out_specs, scratch, flops, moved, *args, limit=VMEM_BYTES):
    return pl.pallas_call(
        kernel,
        out_shape=[jax.ShapeDtypeStruct(s, d) for s, d in out],
        in_specs=in_specs,
        out_specs=out_specs,
        scratch_shapes=scratch,
        compiler_params=params(limit),
        cost_estimate=pl.CostEstimate(flops=flops, bytes_accessed=moved, transcendentals=0),
    )(*args)


def exchange(value):
    return lax.all_to_all(value, "expert", split_axis=0, concat_axis=0, tiled=True)


def pack_call(routes, weight, slot, cap, tokens, cot, count):
    top, n_tokens = routes.shape
    width = tokens.shape[1]
    n_routes, hidden = cot.shape
    part = width + hidden
    rows = 2 * count
    dma = pltpu.SemaphoreType.DMA
    return call(
        pack,
        [((count, 2, 2 * part), BF), ((2, n_routes), jnp.int32), ((1, n_routes), F32)],
        [in_hbm()] * 6,
        [in_hbm(), whole(), whole()],
        [
            pltpu.VMEM((top, n_tokens), jnp.int32),
            pltpu.VMEM((top, n_tokens), F32),
            pltpu.VMEM((1, count), jnp.int32),
            pltpu.VMEM((1, count), jnp.int32),
            pltpu.VMEM((n_tokens, width), BF),
            pltpu.VMEM((n_routes, hidden), BF),
            pltpu.VMEM((count, 2, 2 * part), BF),
            dma((6,)),
            dma((2,)),
        ],
        4 * rows * n_routes * (hidden + 2 * n_tokens),
        4 << 20,
        routes,
        weight,
        slot,
        cap,
        tokens,
        cot,
        limit=VMEM_MOST,
    )


def serve_call(my_cap, recv, own_weights, partner_weights):
    count = recv.shape[0]
    width = own_weights.shape[0]
    hidden = own_weights.shape[1] // 2
    rows = 2 * count
    dma = pltpu.SemaphoreType.DMA
    return call(
        serve_all,
        [((count, 2, 2 * width + TAIL), BF), ((2 * rows, 2 * hidden), BF)],
        [scalars(), whole(), in_hbm(), in_hbm()],
        [whole(), in_hbm()],
        [
            pltpu.VMEM((width, 2 * hidden), BF),
            pltpu.VMEM((width, 2 * hidden), BF),
            pltpu.VMEM((2 * rows, 2 * hidden), BF),
            dma((PIECES + 1,)),
            dma((2,)),
        ],
        16 * rows * width * hidden,
        12 << 20,
        my_cap,
        recv,
        own_weights,
        partner_weights,
        limit=VMEM_SERVE,
    )


def local(tokens, cotangent, routes, route_weight, expert_slot, capacity, gate_up):
    count = lax.axis_size("expert")
    n_tokens, width = tokens.shape
    top = routes.shape[1]
    hidden = cotangent.shape[2]
    n_routes = n_tokens * top
    rows = 2 * count
    my_cap = lax.dynamic_slice(capacity, (lax.axis_index("expert"),), (1,))
    swap = [(s, (s + count // 2) % count) for s in range(count)]

    own_weights = lax.all_gather(gate_up, "dp", axis=1, tiled=True)[0]
    partner_shard = lax.ppermute(gate_up, "expert", swap)
    partner_weights = lax.all_gather(partner_shard, "dp", axis=1, tiled=True)[0]
    send, target, scaled = pack_call(
        routes.T, route_weight.T, expert_slot.reshape(1, count), capacity.reshape(1, count),
        tokens, cotangent.reshape(n_routes, hidden), count,
    )
    recv = exchange(send)
    replicas = lax.axis_size("dp")
    chunk = width // replicas
    send_back, grads = serve_call(my_cap, recv, own_weights, partner_weights)
    back = exchange(send_back)
    all_grads = lax.all_gather(grads, "dp", axis=0, tiled=False)
    me = lax.axis_index("dp").reshape(1)
    received = list(
        call(
            slice_rows,
            [((2 * rows, chunk), BF)] * replicas,
            [scalars(), whole(), in_hbm()],
            [whole()] * replicas,
            [],
            0,
            5 << 20,
            me,
            recv,
            grads,
        )
    )
    for k in range(1, replicas):
        shift = [(q, (q + k) % replicas) for q in range(replicas)]
        received[k] = lax.ppermute(received[k], "dp", shift)
    shard = (chunk, 2 * hidden)
    own_shard, far_shard = call(
        weight_grads,
        [(shard, F32), (shard, BF)],
        [scalars(), scalars()] + [whole()] * 5,
        [whole()] * 2,
        [],
        8 * replicas * rows * chunk * hidden,
        8 << 20,
        my_cap,
        me,
        *received,
        all_grads,
    )
    moved_shard = lax.ppermute(far_shard, "expert", swap)
    gate_up_grad = (own_shard + moved_shard.astype(F32)).astype(BF)[None]

    token_grad, router = call(
        unpack,
        [((n_tokens, width), BF), ((top, n_tokens), F32)],
        [whole()] * 3,
        [whole()] * 2,
        [],
        4 * rows * n_routes * 2 * n_tokens,
        4 << 20,
        target,
        scaled,
        back,
    )
    return token_grad, router.T, gate_up_grad


def solution(mesh):
    in_specs = (
        P(("expert", "dp"), None),
        P(("expert", "dp"), None, None),
        P(("expert", "dp"), None),
        P(("expert", "dp"), None),
        P(),
        P(),
        P("expert", "dp", None),
    )
    out_specs = (P(("expert", "dp"), None), P(("expert", "dp"), None), P("expert", "dp", None))
    return jax.shard_map(local, mesh=mesh, in_specs=in_specs, out_specs=out_specs, check_vma=False)
```

```python
import jax
import jax.numpy as jnp
from jax import lax
from jax.experimental import pallas as pl
from jax.experimental.pallas import tpu as pltpu
from jax.sharding import PartitionSpec as P

BF = jnp.bfloat16
F32 = jnp.float32
VMEM_BYTES = 40 * 1024 * 1024
VMEM_MOST = 56 * 1024 * 1024
TAIL = 128
PIECES = 4
VMEM_SERVE = 47 * 1024 * 1024


def params(limit=VMEM_BYTES):
    return pltpu.CompilerParams(vmem_limit_bytes=limit)


def whole():
    return pl.BlockSpec(memory_space=pltpu.VMEM)


def in_hbm():
    return pl.BlockSpec(memory_space=pltpu.HBM)


def scalars():
    return pl.BlockSpec(memory_space=pltpu.SMEM)


def iota(shape, dim):
    return lax.broadcasted_iota(jnp.int32, shape, dim)


def mm(a, b, ca=1, cb=0):
    return lax.dot_general(a, b, (((ca,), (cb,)), ((), ())), preferred_element_type=F32)


def by_token_and_route(tokens, routes, top):
    shape = (tokens, routes)
    return (iota(shape, 0) == (iota(shape, 1) // top)).astype(BF)


def to_row(per_rank, owner, top):
    routes = owner.shape[1]
    spread = mm(per_rank.astype(F32).astype(BF), owner)
    mine = iota((top, routes), 0) == (iota((top, routes), 1) % top)
    return jnp.sum(jnp.where(mine, spread, 0.0), axis=0, keepdims=True)


def from_row(row, owner, top):
    routes = owner.shape[1]
    mine = iota((top, routes), 0) == (iota((top, routes), 1) % top)
    rest = jnp.where(mine, row, 0.0)
    total = None
    for _ in range(3):
        piece = rest.astype(BF)
        rest = rest - piece.astype(F32)
        term = mm(piece, owner, 1, 1)
        total = term if total is None else total + term
    return total


def copies(sems, *pairs):
    made = [pltpu.make_async_copy(src, dst, sems.at[i]) for i, (src, dst) in enumerate(pairs)]
    for one in made:
        one.start()
    return made


def route_targets(routes_row, owner, slot_row, cap_row):
    experts = slot_row.shape[1]
    tokens, routes = owner.shape
    named = iota((experts, routes), 0) == routes_row
    chosen = mm(named.astype(BF), owner, 1, 1)
    before = (iota((tokens, tokens), 0) < iota((tokens, tokens), 1)).astype(BF)
    earlier = mm(mm(chosen.astype(BF), before).astype(BF), owner)
    rank = jnp.sum(jnp.where(named, earlier, 0.0), axis=0, keepdims=True).astype(jnp.int32)
    square = (experts, experts)
    slot_col = jnp.sum(
        jnp.where(iota(square, 0) == iota(square, 1), slot_row, 0), axis=1, keepdims=True
    )
    cap_col = jnp.sum(jnp.where(iota(square, 1) == slot_col, cap_row, 0), axis=1, keepdims=True)
    slot = jnp.sum(jnp.where(named, slot_col, 0), axis=0, keepdims=True)
    cap = jnp.sum(jnp.where(named, cap_col, 0), axis=0, keepdims=True)
    kept = rank < cap
    far = rank >= 4
    place = jnp.where(far, 7 - rank, rank)
    half = experts // 2
    dest = jnp.where(far, jnp.where(slot >= half, slot - half, slot + half), slot)
    inner = jnp.where(kept & (place < 2), dest * 2 + place, -1)
    outer = jnp.where(kept & (place >= 2), dest * 2 + place - 2, -1)
    return inner, outer


def pack(
    routes_hbm, weight_hbm, slot_hbm, cap_hbm, tokens_hbm, cot_hbm, out_hbm, target_ref, scaled_ref,
    routes, weight, slot, cap, tokens, cot, out, sems, out_sems,
):
    top, n_tokens = routes.shape
    n_routes = top * n_tokens
    width = tokens.shape[1]
    hidden = cot.shape[1]
    part = width + hidden
    loads = copies(
        sems, (routes_hbm, routes), (slot_hbm, slot), (cap_hbm, cap), (weight_hbm, weight),
        (tokens_hbm, tokens), (cot_hbm, cot),
    )
    owner = by_token_and_route(n_tokens, n_routes, top)
    for one in loads[:4]:
        one.wait()
    routes_row = to_row(routes[...], owner, top).astype(jnp.int32)
    weight_row = to_row(weight[...], owner, top)
    scaled_ref[...] = weight_row
    targets = route_targets(routes_row, owner, slot[...], cap[...])
    target_ref[0:1, :] = targets[0]
    target_ref[1:2, :] = targets[1]
    rows = out.shape[0] * out.shape[1]
    stores = []

    def send(span):
        sem = out_sems.at[len(stores)]
        store = pltpu.make_async_copy(out.at[:, :, span], out_hbm.at[:, :, span], sem)
        store.start()
        stores.append(store)

    loads[4].wait()
    for i, target in enumerate(targets):
        hit = iota((rows, n_routes), 0) == target
        pick = mm(hit.astype(BF), owner, 1, 1).astype(BF)
        start = i * part
        moved = mm(pick, tokens[...]).astype(BF)
        out[:, :, start : start + width] = moved.reshape(rows // 2, 2, width)
        send(pl.ds(start, width))
        if i == 0:
            loads[5].wait()
        moved = mm(jnp.where(hit, weight_row, 0.0).astype(BF), cot[...]).astype(BF)
        out[:, :, start + width : start + part] = moved.reshape(rows // 2, 2, hidden)
        send(pl.ds(start + width, hidden))
    for one in stores:
        one.wait()


def split_router(router, lane):
    high = router.astype(BF).astype(F32)
    low = router - high
    lanes = iota((router.shape[0], TAIL), 1)
    return jnp.where(lanes == lane, high, jnp.where(lanes == lane + 1, low, 0.0))


def serve(rows, scaled, weights, loads):
    width, hidden = weights.shape[0], weights.shape[1] // 2
    pre = None
    deep = width // len(loads)
    for k, load in enumerate(loads):
        load.wait()
        span = slice(k * deep, (k + 1) * deep)
        term = mm(rows[:, span], weights[span, :])
        pre = term if pre is None else pre + term
    scaled = scaled.astype(F32)
    gate = pre[:, :hidden]
    up = pre[:, hidden:]
    sig = jax.nn.sigmoid(gate)
    active = gate * sig
    grad_up = scaled * active
    grad_gate = scaled * up * sig * (1.0 + gate * (1.0 - sig))
    grad = jnp.concatenate([grad_gate, grad_up], axis=1).astype(BF)
    router = jnp.sum(grad_up * up, axis=1, keepdims=True)
    back = mm(grad, weights[...], 1, 1).astype(BF)
    return grad, router, back


def serve_all(
    cap_ref, recv, own_hbm, partner_hbm, back, rows_hbm, grad_hbm,
    own, other, all_rows, all_grads, sems, out_sems,
):
    width = own.shape[0]
    hidden = own.shape[1] // 2
    part = width + hidden
    sources = recv.shape[0]
    rows = 2 * sources
    chunks, _, chunk = all_rows.shape
    is_own = cap_ref[0] > 2
    deep = width // PIECES
    pieces = [pl.ds(k * deep, deep) for k in range(PIECES)]
    loads = copies(sems, *[(own_hbm.at[p], own.at[p]) for p in pieces])
    last = sems.at[PIECES]

    @pl.when(is_own)
    def _():
        pltpu.make_async_copy(own_hbm, other, last).start()

    @pl.when(jnp.logical_not(is_own))
    def _():
        pltpu.make_async_copy(partner_hbm, other, last).start()

    ready = (loads, [pltpu.make_async_copy(own_hbm, other, last)])
    stores = []

    def store(src, dst):
        one = pltpu.make_async_copy(src, dst, out_sems.at[len(stores)])
        one.start()
        stores.append(one)

    tail = None
    for i, weights in enumerate((own, other)):
        start = i * part
        span = pl.ds(i * rows, rows)
        tokens = recv[:, :, start : start + width].reshape(rows, width)
        for c in range(chunks):
            all_rows[c, i * rows : (i + 1) * rows, :] = tokens[:, c * chunk : (c + 1) * chunk]
        store(all_rows.at[:, span, :], rows_hbm.at[pl.ds(0, chunks), span, :])
        scaled = recv[:, :, start + width : start + part].reshape(rows, hidden)
        grad, router, result = serve(tokens, scaled, weights, ready[i])
        all_grads[i * rows : (i + 1) * rows, :] = grad
        store(all_grads.at[span], grad_hbm.at[span])
        back[:, :, i * width : (i + 1) * width] = result.reshape(sources, 2, width)
        lanes = split_router(router, 2 * i)
        tail = lanes if tail is None else tail + lanes
    back[:, :, 2 * width :] = tail.astype(BF).reshape(sources, 2, TAIL)
    for one in stores:
        one.wait()


def weight_grads(cap_ref, me_ref, rows_0, rows_1, rows_2, rows_3, grads, own_ref, far_ref):
    received = (rows_0, rows_1, rows_2, rows_3)
    sources = len(received)
    half = rows_0.shape[0] // 2
    is_own = cap_ref[0] > 2
    inner = None
    outer = None
    for k, rows in enumerate(received):
        source = lax.rem(me_ref[0] + sources - k, sources)
        term = mm(rows[:half, :], grads[source, :half, :], 0, 0)
        inner = term if inner is None else inner + term
        term = mm(rows[half:, :], grads[source, half:, :], 0, 0)
        outer = term if outer is None else outer + term
    own_ref[...] = inner + jnp.where(is_own, outer, 0.0)
    far_ref[...] = jnp.where(is_own, 0.0, outer).astype(BF)


def unpack(target_ref, scaled_ref, back, token_ref, router_ref):
    n_tokens, width = token_ref.shape
    top = router_ref.shape[0]
    n_routes = top * n_tokens
    rows = 2 * back.shape[0]
    owner = by_token_and_route(n_tokens, n_routes, top)
    hits = [
        (iota((rows, n_routes), 0) == target_ref[i : i + 1, :]).astype(BF) for i in range(2)
    ]
    picks = [mm(owner, hit, 1, 1).astype(BF) for hit in hits]
    tail = back[:, :, 2 * width :].reshape(rows, TAIL)
    router = None
    for i, hit in enumerate(hits):
        found = mm(tail, hit, 0, 0)
        value = found[2 * i : 2 * i + 1, :] + found[2 * i + 1 : 2 * i + 2, :]
        router = value if router is None else router + value
    router_ref[...] = from_row(router / scaled_ref[...], owner, top)
    total = None
    for i, pick in enumerate(picks):
        term = mm(pick, back[:, :, i * width : (i + 1) * width].reshape(rows, width))
        total = term if total is None else total + term
    token_ref[...] = total.astype(BF)


def call(kernel, out, in_specs, out_specs, scratch, flops, moved, *args, limit=VMEM_BYTES):
    return pl.pallas_call(
        kernel,
        out_shape=[jax.ShapeDtypeStruct(s, d) for s, d in out],
        in_specs=in_specs,
        out_specs=out_specs,
        scratch_shapes=scratch,
        compiler_params=params(limit),
        cost_estimate=pl.CostEstimate(flops=flops, bytes_accessed=moved, transcendentals=0),
    )(*args)


def exchange(value):
    return lax.all_to_all(value, "expert", split_axis=0, concat_axis=0, tiled=True)


def pack_call(routes, weight, slot, cap, tokens, cot, count):
    top, n_tokens = routes.shape
    width = tokens.shape[1]
    n_routes, hidden = cot.shape
    part = width + hidden
    rows = 2 * count
    dma = pltpu.SemaphoreType.DMA
    return call(
        pack,
        [((count, 2, 2 * part), BF), ((2, n_routes), jnp.int32), ((1, n_routes), F32)],
        [in_hbm()] * 6,
        [in_hbm(), whole(), whole()],
        [
            pltpu.VMEM((top, n_tokens), jnp.int32),
            pltpu.VMEM((top, n_tokens), F32),
            pltpu.VMEM((1, count), jnp.int32),
            pltpu.VMEM((1, count), jnp.int32),
            pltpu.VMEM((n_tokens, width), BF),
            pltpu.VMEM((n_routes, hidden), BF),
            pltpu.VMEM((count, 2, 2 * part), BF),
            dma((6,)),
            dma((4,)),
        ],
        4 * rows * n_routes * (hidden + 2 * n_tokens),
        4 << 20,
        routes,
        weight,
        slot,
        cap,
        tokens,
        cot,
        limit=VMEM_MOST,
    )


def serve_call(my_cap, recv, own_weights, partner_weights, replicas):
    count = recv.shape[0]
    width = own_weights.shape[0]
    hidden = own_weights.shape[1] // 2
    rows = 2 * count
    chunk = width // replicas
    dma = pltpu.SemaphoreType.DMA
    return call(
        serve_all,
        [
            ((count, 2, 2 * width + TAIL), BF),
            ((2 * replicas, 2 * rows, chunk), BF),
            ((2 * rows, 2 * hidden), BF),
        ],
        [scalars(), whole(), in_hbm(), in_hbm()],
        [whole(), in_hbm(), in_hbm()],
        [
            pltpu.VMEM((width, 2 * hidden), BF),
            pltpu.VMEM((width, 2 * hidden), BF),
            pltpu.VMEM((replicas, 2 * rows, chunk), BF),
            pltpu.VMEM((2 * rows, 2 * hidden), BF),
            dma((PIECES + 1,)),
            dma((4,)),
        ],
        16 * rows * width * hidden,
        12 << 20,
        my_cap,
        recv,
        own_weights,
        partner_weights,
        limit=VMEM_SERVE,
    )


def local(tokens, cotangent, routes, route_weight, expert_slot, capacity, gate_up):
    count = lax.axis_size("expert")
    n_tokens, width = tokens.shape
    top = routes.shape[1]
    hidden = cotangent.shape[2]
    n_routes = n_tokens * top
    rows = 2 * count
    my_cap = lax.dynamic_slice(capacity, (lax.axis_index("expert"),), (1,))
    swap = [(s, (s + count // 2) % count) for s in range(count)]

    own_weights = lax.all_gather(gate_up, "dp", axis=1, tiled=True)[0]
    partner_shard = lax.ppermute(gate_up, "expert", swap)
    partner_weights = lax.all_gather(partner_shard, "dp", axis=1, tiled=True)[0]
    send, target, scaled = pack_call(
        routes.T, route_weight.T, expert_slot.reshape(1, count), capacity.reshape(1, count),
        tokens, cotangent.reshape(n_routes, hidden), count,
    )
    recv = exchange(send)
    replicas = lax.axis_size("dp")
    chunk = width // replicas
    send_back, sent_rows, grads = serve_call(
        my_cap, recv, own_weights, partner_weights, replicas
    )
    back = exchange(send_back)
    all_grads = lax.all_gather(grads, "dp", axis=0, tiled=False)
    me = lax.axis_index("dp")
    received = []
    for k in range(replicas):
        piece = lax.dynamic_index_in_dim(
            sent_rows, lax.rem(me + k, replicas), axis=0, keepdims=False
        )
        if k:
            piece = lax.ppermute(piece, "dp", [(q, (q + k) % replicas) for q in range(replicas)])
        received.append(piece)
    shard = (chunk, 2 * hidden)
    own_shard, far_shard = call(
        weight_grads,
        [(shard, F32), (shard, BF)],
        [scalars(), scalars()] + [whole()] * 5,
        [whole()] * 2,
        [],
        8 * replicas * rows * chunk * hidden,
        8 << 20,
        my_cap,
        me.reshape(1),
        *received,
        all_grads,
    )
    moved_shard = lax.ppermute(far_shard, "expert", swap)
    gate_up_grad = (own_shard + moved_shard.astype(F32)).astype(BF)[None]

    token_grad, router = call(
        unpack,
        [((n_tokens, width), BF), ((top, n_tokens), F32)],
        [whole()] * 3,
        [whole()] * 2,
        [],
        4 * rows * n_routes * 2 * n_tokens,
        4 << 20,
        target,
        scaled,
        back,
    )
    return token_grad, router.T, gate_up_grad


def solution(mesh):
    in_specs = (
        P(("expert", "dp"), None),
        P(("expert", "dp"), None, None),
        P(("expert", "dp"), None),
        P(("expert", "dp"), None),
        P(),
        P(),
        P("expert", "dp", None),
    )
    out_specs = (P(("expert", "dp"), None), P(("expert", "dp"), None), P("expert", "dp", None))
    return jax.shard_map(local, mesh=mesh, in_specs=in_specs, out_specs=out_specs, check_vma=False)
```

```python
import jax
import jax.numpy as jnp
from jax import lax
from jax.experimental import pallas as pl
from jax.experimental.pallas import tpu as pltpu
from jax.sharding import PartitionSpec as P

BF = jnp.bfloat16
F32 = jnp.float32
VMEM_BYTES = 40 * 1024 * 1024
VMEM_MOST = 56 * 1024 * 1024
TAIL = 128
PIECES = 2
VMEM_SERVE = 47 * 1024 * 1024


def params(limit=VMEM_BYTES):
    return pltpu.CompilerParams(vmem_limit_bytes=limit)


def whole():
    return pl.BlockSpec(memory_space=pltpu.VMEM)


def in_hbm():
    return pl.BlockSpec(memory_space=pltpu.HBM)


def scalars():
    return pl.BlockSpec(memory_space=pltpu.SMEM)


def iota(shape, dim):
    return lax.broadcasted_iota(jnp.int32, shape, dim)


def mm(a, b, ca=1, cb=0):
    return lax.dot_general(a, b, (((ca,), (cb,)), ((), ())), preferred_element_type=F32)


def by_token_and_route(tokens, routes, top):
    shape = (tokens, routes)
    return (iota(shape, 0) == (iota(shape, 1) // top)).astype(BF)


def to_row(per_rank, owner, top):
    routes = owner.shape[1]
    spread = mm(per_rank.astype(F32).astype(BF), owner)
    mine = iota((top, routes), 0) == (iota((top, routes), 1) % top)
    return jnp.sum(jnp.where(mine, spread, 0.0), axis=0, keepdims=True)


def from_row(row, owner, top):
    routes = owner.shape[1]
    mine = iota((top, routes), 0) == (iota((top, routes), 1) % top)
    rest = jnp.where(mine, row, 0.0)
    total = None
    for _ in range(3):
        piece = rest.astype(BF)
        rest = rest - piece.astype(F32)
        term = mm(piece, owner, 1, 1)
        total = term if total is None else total + term
    return total


def copies(sems, *pairs):
    made = [pltpu.make_async_copy(src, dst, sems.at[i]) for i, (src, dst) in enumerate(pairs)]
    for one in made:
        one.start()
    return made


def route_targets(routes_row, owner, slot_row, cap_row):
    experts = slot_row.shape[1]
    tokens, routes = owner.shape
    named = iota((experts, routes), 0) == routes_row
    chosen = mm(named.astype(BF), owner, 1, 1)
    before = (iota((tokens, tokens), 0) < iota((tokens, tokens), 1)).astype(BF)
    earlier = mm(mm(chosen.astype(BF), before).astype(BF), owner)
    rank = jnp.sum(jnp.where(named, earlier, 0.0), axis=0, keepdims=True).astype(jnp.int32)
    square = (experts, experts)
    slot_col = jnp.sum(
        jnp.where(iota(square, 0) == iota(square, 1), slot_row, 0), axis=1, keepdims=True
    )
    cap_col = jnp.sum(jnp.where(iota(square, 1) == slot_col, cap_row, 0), axis=1, keepdims=True)
    slot = jnp.sum(jnp.where(named, slot_col, 0), axis=0, keepdims=True)
    cap = jnp.sum(jnp.where(named, cap_col, 0), axis=0, keepdims=True)
    kept = rank < cap
    far = rank >= 4
    place = jnp.where(far, 7 - rank, rank)
    half = experts // 2
    dest = jnp.where(far, jnp.where(slot >= half, slot - half, slot + half), slot)
    inner = jnp.where(kept & (place < 2), dest * 2 + place, -1)
    outer = jnp.where(kept & (place >= 2), dest * 2 + place - 2, -1)
    return inner, outer


def pack(
    routes_hbm, weight_hbm, slot_hbm, cap_hbm, tokens_hbm, cot_hbm, out_hbm, target_ref, scaled_ref,
    routes, weight, slot, cap, tokens, cot, out, sems, out_sems,
):
    top, n_tokens = routes.shape
    n_routes = top * n_tokens
    width = tokens.shape[1]
    hidden = cot.shape[1]
    part = width + hidden
    loads = copies(
        sems, (routes_hbm, routes), (slot_hbm, slot), (cap_hbm, cap), (weight_hbm, weight),
        (tokens_hbm, tokens), (cot_hbm, cot),
    )
    owner = by_token_and_route(n_tokens, n_routes, top)
    for one in loads[:4]:
        one.wait()
    routes_row = to_row(routes[...], owner, top).astype(jnp.int32)
    weight_row = to_row(weight[...], owner, top)
    scaled_ref[...] = weight_row
    targets = route_targets(routes_row, owner, slot[...], cap[...])
    target_ref[0:1, :] = targets[0]
    target_ref[1:2, :] = targets[1]
    rows = out.shape[0] * out.shape[1]
    stores = []

    def send(span):
        sem = out_sems.at[len(stores)]
        store = pltpu.make_async_copy(out.at[:, :, span], out_hbm.at[:, :, span], sem)
        store.start()
        stores.append(store)

    for i, target in enumerate(targets):
        hit = iota((rows, n_routes), 0) == target
        pick = mm(hit.astype(BF), owner, 1, 1).astype(BF)
        if i == 0:
            loads[4].wait()
        start = i * part
        moved = mm(pick, tokens[...]).astype(BF)
        out[:, :, start : start + width] = moved.reshape(rows // 2, 2, width)
        send(pl.ds(start, width))
        if i == 0:
            loads[5].wait()
        moved = mm(jnp.where(hit, weight_row, 0.0).astype(BF), cot[...]).astype(BF)
        out[:, :, start + width : start + part] = moved.reshape(rows // 2, 2, hidden)
        send(pl.ds(start + width, hidden))
    for one in stores:
        one.wait()


def split_router(router, lane):
    high = router.astype(BF).astype(F32)
    low = router - high
    lanes = iota((router.shape[0], TAIL), 1)
    return jnp.where(lanes == lane, high, jnp.where(lanes == lane + 1, low, 0.0))


def serve(rows, scaled, weights, loads):
    width, hidden = weights.shape[0], weights.shape[1] // 2
    pre = None
    deep = width // len(loads)
    for k, load in enumerate(loads):
        load.wait()
        span = slice(k * deep, (k + 1) * deep)
        term = mm(rows[:, span], weights[span, :])
        pre = term if pre is None else pre + term
    scaled = scaled.astype(F32)
    gate = pre[:, :hidden]
    up = pre[:, hidden:]
    sig = jax.nn.sigmoid(gate)
    active = gate * sig
    grad_up = scaled * active
    grad_gate = scaled * up * sig * (1.0 + gate * (1.0 - sig))
    grad = jnp.concatenate([grad_gate, grad_up], axis=1).astype(BF)
    router = jnp.sum(grad_up * up, axis=1, keepdims=True)
    back = mm(grad, weights[...], 1, 1).astype(BF)
    return grad, router, back


def serve_all(
    cap_ref, recv, own_hbm, partner_hbm, back, rows_hbm, grad_hbm,
    own, other, all_rows, all_grads, sems, out_sems,
):
    width = own.shape[0]
    hidden = own.shape[1] // 2
    part = width + hidden
    sources = recv.shape[0]
    rows = 2 * sources
    chunks, _, chunk = all_rows.shape
    is_own = cap_ref[0] > 2
    deep = width // PIECES
    pieces = [pl.ds(k * deep, deep) for k in range(PIECES)]
    loads = copies(sems, *[(own_hbm.at[p], own.at[p]) for p in pieces])
    last = sems.at[PIECES]

    @pl.when(is_own)
    def _():
        pltpu.make_async_copy(own_hbm, other, last).start()

    @pl.when(jnp.logical_not(is_own))
    def _():
        pltpu.make_async_copy(partner_hbm, other, last).start()

    ready = (loads, [pltpu.make_async_copy(own_hbm, other, last)])
    stores = []

    def store(src, dst):
        one = pltpu.make_async_copy(src, dst, out_sems.at[len(stores)])
        one.start()
        stores.append(one)

    parts = []
    for i in range(2):
        start = i * part
        span = pl.ds(i * rows, rows)
        tokens = recv[:, :, start : start + width].reshape(rows, width)
        for c in range(chunks):
            all_rows[c, i * rows : (i + 1) * rows, :] = tokens[:, c * chunk : (c + 1) * chunk]
        store(all_rows.at[:, span, :], rows_hbm.at[pl.ds(0, chunks), span, :])
        scaled = recv[:, :, start + width : start + part].reshape(rows, hidden)
        parts.append((tokens, scaled))
    tail = None
    for i, weights in enumerate((own, other)):
        span = pl.ds(i * rows, rows)
        tokens, scaled = parts[i]
        grad, router, result = serve(tokens, scaled, weights, ready[i])
        all_grads[i * rows : (i + 1) * rows, :] = grad
        store(all_grads.at[span], grad_hbm.at[span])
        back[:, :, i * width : (i + 1) * width] = result.reshape(sources, 2, width)
        lanes = split_router(router, 2 * i)
        tail = lanes if tail is None else tail + lanes
    back[:, :, 2 * width :] = tail.astype(BF).reshape(sources, 2, TAIL)
    for one in stores:
        one.wait()


def weight_grads(cap_ref, me_ref, rows_0, rows_1, rows_2, rows_3, grads, own_ref, far_ref):
    received = (rows_0, rows_1, rows_2, rows_3)
    sources = len(received)
    half = rows_0.shape[0] // 2
    is_own = cap_ref[0] > 2
    inner = None
    outer = None
    for k, rows in enumerate(received):
        source = lax.rem(me_ref[0] + sources - k, sources)
        term = mm(rows[:half, :], grads[source, :half, :], 0, 0)
        inner = term if inner is None else inner + term
        term = mm(rows[half:, :], grads[source, half:, :], 0, 0)
        outer = term if outer is None else outer + term
    own_ref[...] = inner + jnp.where(is_own, outer, 0.0)
    far_ref[...] = jnp.where(is_own, 0.0, outer).astype(BF)


def unpack(target_ref, scaled_ref, back, token_ref, router_ref):
    n_tokens, width = token_ref.shape
    top = router_ref.shape[0]
    n_routes = top * n_tokens
    rows = 2 * back.shape[0]
    owner = by_token_and_route(n_tokens, n_routes, top)
    hits = [
        (iota((rows, n_routes), 0) == target_ref[i : i + 1, :]).astype(BF) for i in range(2)
    ]
    picks = [mm(owner, hit, 1, 1).astype(BF) for hit in hits]
    tail = back[:, :, 2 * width :].reshape(rows, TAIL)
    router = None
    for i, hit in enumerate(hits):
        found = mm(tail, hit, 0, 0)
        value = found[2 * i : 2 * i + 1, :] + found[2 * i + 1 : 2 * i + 2, :]
        router = value if router is None else router + value
    router_ref[...] = from_row(router / scaled_ref[...], owner, top)
    total = None
    for i, pick in enumerate(picks):
        term = mm(pick, back[:, :, i * width : (i + 1) * width].reshape(rows, width))
        total = term if total is None else total + term
    token_ref[...] = total.astype(BF)


def call(kernel, out, in_specs, out_specs, scratch, flops, moved, *args, limit=VMEM_BYTES):
    return pl.pallas_call(
        kernel,
        out_shape=[jax.ShapeDtypeStruct(s, d) for s, d in out],
        in_specs=in_specs,
        out_specs=out_specs,
        scratch_shapes=scratch,
        compiler_params=params(limit),
        cost_estimate=pl.CostEstimate(flops=flops, bytes_accessed=moved, transcendentals=0),
    )(*args)


def exchange(value):
    return lax.all_to_all(value, "expert", split_axis=0, concat_axis=0, tiled=True)


def pack_call(routes, weight, slot, cap, tokens, cot, count):
    top, n_tokens = routes.shape
    width = tokens.shape[1]
    n_routes, hidden = cot.shape
    part = width + hidden
    rows = 2 * count
    dma = pltpu.SemaphoreType.DMA
    return call(
        pack,
        [((count, 2, 2 * part), BF), ((2, n_routes), jnp.int32), ((1, n_routes), F32)],
        [in_hbm()] * 6,
        [in_hbm(), whole(), whole()],
        [
            pltpu.VMEM((top, n_tokens), jnp.int32),
            pltpu.VMEM((top, n_tokens), F32),
            pltpu.VMEM((1, count), jnp.int32),
            pltpu.VMEM((1, count), jnp.int32),
            pltpu.VMEM((n_tokens, width), BF),
            pltpu.VMEM((n_routes, hidden), BF),
            pltpu.VMEM((count, 2, 2 * part), BF),
            dma((6,)),
            dma((4,)),
        ],
        4 * rows * n_routes * (hidden + 2 * n_tokens),
        4 << 20,
        routes,
        weight,
        slot,
        cap,
        tokens,
        cot,
        limit=VMEM_MOST,
    )


def serve_call(my_cap, recv, own_weights, partner_weights, replicas):
    count = recv.shape[0]
    width = own_weights.shape[0]
    hidden = own_weights.shape[1] // 2
    rows = 2 * count
    chunk = width // replicas
    dma = pltpu.SemaphoreType.DMA
    return call(
        serve_all,
        [
            ((count, 2, 2 * width + TAIL), BF),
            ((2 * replicas, 2 * rows, chunk), BF),
            ((2 * rows, 2 * hidden), BF),
        ],
        [scalars(), whole(), in_hbm(), in_hbm()],
        [whole(), in_hbm(), in_hbm()],
        [
            pltpu.VMEM((width, 2 * hidden), BF),
            pltpu.VMEM((width, 2 * hidden), BF),
            pltpu.VMEM((replicas, 2 * rows, chunk), BF),
            pltpu.VMEM((2 * rows, 2 * hidden), BF),
            dma((PIECES + 1,)),
            dma((4,)),
        ],
        16 * rows * width * hidden,
        12 << 20,
        my_cap,
        recv,
        own_weights,
        partner_weights,
        limit=VMEM_SERVE,
    )


def local(tokens, cotangent, routes, route_weight, expert_slot, capacity, gate_up):
    count = lax.axis_size("expert")
    n_tokens, width = tokens.shape
    top = routes.shape[1]
    hidden = cotangent.shape[2]
    n_routes = n_tokens * top
    rows = 2 * count
    my_cap = lax.dynamic_slice(capacity, (lax.axis_index("expert"),), (1,))
    swap = [(s, (s + count // 2) % count) for s in range(count)]

    own_weights = lax.all_gather(gate_up, "dp", axis=1, tiled=True)[0]
    partner_shard = lax.ppermute(gate_up, "expert", swap)
    partner_weights = lax.all_gather(partner_shard, "dp", axis=1, tiled=True)[0]
    send, target, scaled = pack_call(
        routes.T, route_weight.T, expert_slot.reshape(1, count), capacity.reshape(1, count),
        tokens, cotangent.reshape(n_routes, hidden), count,
    )
    recv = exchange(send)
    replicas = lax.axis_size("dp")
    chunk = width // replicas
    send_back, sent_rows, grads = serve_call(
        my_cap, recv, own_weights, partner_weights, replicas
    )
    back = exchange(send_back)
    all_grads = lax.all_gather(grads, "dp", axis=0, tiled=False)
    me = lax.axis_index("dp")
    received = []
    for k in range(replicas):
        piece = lax.dynamic_index_in_dim(
            sent_rows, lax.rem(me + k, replicas), axis=0, keepdims=False
        )
        if k:
            piece = lax.ppermute(piece, "dp", [(q, (q + k) % replicas) for q in range(replicas)])
        received.append(piece)
    shard = (chunk, 2 * hidden)
    own_shard, far_shard = call(
        weight_grads,
        [(shard, F32), (shard, BF)],
        [scalars(), scalars()] + [whole()] * 5,
        [whole()] * 2,
        [],
        8 * replicas * rows * chunk * hidden,
        8 << 20,
        my_cap,
        me.reshape(1),
        *received,
        all_grads,
    )
    moved_shard = lax.ppermute(far_shard, "expert", swap)
    gate_up_grad = (own_shard + moved_shard.astype(F32)).astype(BF)[None]

    token_grad, router = call(
        unpack,
        [((n_tokens, width), BF), ((top, n_tokens), F32)],
        [whole()] * 3,
        [whole()] * 2,
        [],
        4 * rows * n_routes * 2 * n_tokens,
        4 << 20,
        target,
        scaled,
        back,
    )
    return token_grad, router.T, gate_up_grad


def solution(mesh):
    in_specs = (
        P(("expert", "dp"), None),
        P(("expert", "dp"), None, None),
        P(("expert", "dp"), None),
        P(("expert", "dp"), None),
        P(),
        P(),
        P("expert", "dp", None),
    )
    out_specs = (P(("expert", "dp"), None), P(("expert", "dp"), None), P("expert", "dp", None))
    return jax.shard_map(local, mesh=mesh, in_specs=in_specs, out_specs=out_specs, check_vma=False)
```
